32 devices in a mesh: seq: 8 (over y, x, core), dp: 4 (over z).
Axes of the slice: x: 2, y: 2, z: 4, core: 2. Of those that a mesh axis runs over, the one named last changes fastest.
Arguments:
- queries: bfloat16 [4, 1024, 2048], P('dp', 'seq'), may hold values from -6 to 6
- keys_in: bfloat16 [4, 1024, 2048], P('dp', 'seq'), may hold values from -9 to 9
- values_in: bfloat16 [4, 1024, 2048], P('dp', 'seq'), may hold values from -6 to 6
- inputs: bfloat16 [4, 1024, 2048], P('dp', 'seq'), may hold values from -6 to 6
- target: bfloat16 [4, 1024, 2048], P('dp', 'seq'), may hold values from -4 to 4
- gate_weight: bfloat16 [2048, 16], replicated, may hold values from -0.125 to 0.125
- beta_bias: float32 [16], replicated, may hold values from -9 to 1.5
Outputs:
- output: bfloat16 [4, 1024, 2048], P('dp', 'seq')
- grad_queries: bfloat16 [4, 1024, 2048], P('dp', 'seq')
- grad_keys: bfloat16 [4, 1024, 2048], P('dp', 'seq')
- grad_values: bfloat16 [4, 1024, 2048], P('dp', 'seq')
- grad_weight: float32 [2048, 16], replicated
The draws below stay inside these ranges and needn't reach their ends.
All inputs are finite; a program needn't handle non-finite values.
Results may differ from the reference program's by a relative error of at most 0.0035.
Values sent between devices are 32-bit elements; how exact they have to be, the bound alone decides.
No kernel may reach another device: no remote copies, remote signals or barrier semaphores. Data moves between devices by JAX's collectives and lax.ppermute only.
A program may use at most 256 MiB of HBM per device.

```python
import math
import jax
import jax.numpy as jnp
from jax import lax

HEADS = 16
DK = 128
D = 2048
BLOCK = 128
SEQLEN = 1024
SEQS = 4


def draw_beta_bias(key, part):
    key = jax.random.fold_in(key, 5)
    ranking = jax.random.permutation(jax.random.fold_in(key, 11), HEADS)
    spread = jax.random.uniform(jax.random.fold_in(key, 12), (HEADS,), jnp.float32)
    fast_rate = 0.2 + 0.2 * spread
    slow_rate = DK * 0.6 * jnp.exp(spread * math.log(5.0)) / SEQLEN
    slow_heads = ranking < HEADS // 2
    slow_rate = jnp.minimum(slow_rate, 0.4)
    decay_rate = jnp.where(slow_heads, slow_rate, fast_rate).astype(jnp.float32)
    return jnp.log(2.0 * decay_rate) - jnp.log(1.0 - 2.0 * decay_rate)


def draw_keys_in(key, part):
    key = jax.random.fold_in(key, 21)
    shared = jnp.clip(jax.random.normal(jax.random.fold_in(key, 1), (SEQS, 1, D), jnp.float32), -3.0, 3.0)
    noise = jnp.clip(jax.random.normal(jax.random.fold_in(key, 2), (SEQS, SEQLEN, D), jnp.float32), -4.0, 4.0)
    amplitude = 1.5
    return (amplitude * shared + noise).astype(jnp.bfloat16)


def block_scale(own_key, dims, cuts, smallest, high):
    def one(axis_at, shards_of):
        heights = jax.random.uniform(jax.random.fold_in(jax.random.fold_in(own_key, 6), axis_at), (shards_of,), jnp.float32, smallest / len(cuts), high / len(cuts))
        return jnp.repeat(jnp.exp(heights), dims[axis_at] // shards_of).reshape((-1,) + (1,) * (len(dims) - axis_at - 1))

    factor_of = one(*cuts[0])
    for cut in cuts[1:]:
        factor_of = factor_of * one(*cut)
    return factor_of


def centred(key, dims, scale, limit, cuts=(), kind=jnp.bfloat16):
    loudness = block_scale(key, dims, cuts, -0.22, 0.18) if cuts else 1.0
    drawn = jax.random.normal(key, dims, jnp.float32) * scale * loudness
    return jnp.minimum(jnp.maximum(drawn, -limit), limit).astype(kind)


def setup_inputs(seed: int = 0) -> dict:
    key_list = jax.random.split(jax.random.key(seed), 8)
    queries = centred(key_list[0], (SEQS, SEQLEN, D), 1.0, 6.0, ((0, 4), (1, 8)))
    keys_in = draw_keys_in(jax.random.fold_in(key_list[7], 71), 0)
    values_in = centred(key_list[2], (SEQS, SEQLEN, D), 1.0, 6.0, ((0, 4), (1, 8)))
    inputs = centred(key_list[3], (SEQS, SEQLEN, D), 1.0, 6.0, ((0, 4), (1, 8)))
    target = centred(key_list[4], (SEQS, SEQLEN, D), 0.5, 4.0, ((0, 4), (1, 8)))
    gate_weight = centred(key_list[5], (D, HEADS), D ** -0.5, 0.125)
    beta_bias = draw_beta_bias(jax.random.fold_in(key_list[7], 71), 0)
    return dict(queries=queries, keys_in=keys_in, values_in=values_in, inputs=inputs, target=target, gate_weight=gate_weight, beta_bias=beta_bias)


epsilon = 1e-06
highest_precision = lax.Precision.HIGHEST

def unit_rows(matrix):
    return matrix * lax.rsqrt(lax.optimization_barrier(jnp.sum(matrix * matrix, axis=-1, keepdims=True)) + epsilon)

def block_terms(queries, keys_in, values_in, logits):
    length = queries.shape[0]
    head_count = logits.shape[1]
    head_width = queries.shape[1] // head_count
    blocks = length // BLOCK

    def arrange(matrix):
        return matrix.reshape(blocks, BLOCK, head_count, head_width).transpose(0, 2, 1, 3)
    query_unit = unit_rows(arrange(queries.astype(jnp.float32)))
    key_unit = unit_rows(arrange(keys_in.astype(jnp.float32)))
    value_rows = arrange(values_in.astype(jnp.float32))
    strength = (0.5 * jax.nn.sigmoid(logits)).reshape(blocks, BLOCK, head_count).transpose(0, 2, 1)[..., None]
    key_gram = jnp.einsum('nhik,nhjk->nhij', key_unit, key_unit, precision=highest_precision)
    lower_mask = jnp.tril(jnp.ones((BLOCK, BLOCK), jnp.float32), -1)
    system = jnp.eye(BLOCK, dtype=jnp.float32) + lower_mask * strength * key_gram
    right_side = jnp.concatenate([strength * key_unit, strength * value_rows], axis=-1)
    solved = jax.scipy.linalg.solve_triangular(system, right_side, lower=True)
    write_keys = solved[..., :head_width]
    write_values = solved[..., head_width:]
    inclusive = jnp.tril(jnp.ones((BLOCK, BLOCK), jnp.float32))
    scores = inclusive * jnp.einsum('nhik,nhjk->nhij', query_unit, key_unit, precision=highest_precision)
    return (query_unit, key_unit, write_keys, write_values, scores)

def state_pass(terms, entry_state):

    def advance(carried_state, block_parts):
        block_queries, block_keys, write_keys, write_values, score_block = block_parts
        delta_correction = write_values - jnp.einsum('fbi,fir->fbr', write_keys, carried_state, precision=highest_precision)
        produced_output = jnp.einsum('fbi,fir->fbr', block_queries, carried_state, precision=highest_precision)
        produced_output = produced_output + jnp.einsum('hcj,hjv->hcv', score_block, delta_correction, precision=highest_precision)
        carried_state = carried_state + jnp.einsum('nrm,nrp->nmp', block_keys, delta_correction, precision=highest_precision)
        return (carried_state, produced_output)
    final_state, produced_output = lax.scan(advance, entry_state, terms)
    blocks, head_count, rows_block, head_width = produced_output.shape
    flat = produced_output.transpose(0, 2, 1, 3).reshape(blocks * rows_block, head_count * head_width)
    return (flat, final_state)

def one_sequence(queries, keys_in, values_in, inputs, target, gate_weight, beta_bias):
    head_count = gate_weight.shape[1]
    head_width = queries.shape[1] // head_count
    logits = jnp.dot(inputs.astype(jnp.float32), gate_weight.astype(jnp.float32), preferred_element_type=jnp.float32) + beta_bias

    def forward(queries, keys_in, values_in, logits):
        terms = block_terms(queries, keys_in, values_in, logits)
        entry_state = jnp.zeros((head_count, head_width, head_width), jnp.float32)
        return state_pass(terms, entry_state)[0]
    produced_output, pullback = jax.vjp(forward, queries, keys_in, values_in, logits)
    rounded = lax.optimization_barrier(produced_output.astype(jnp.bfloat16))
    cotangent = rounded.astype(jnp.float32) - target.astype(jnp.float32)
    grad_q, grad_k, grad_v, grad_logits = pullback(cotangent)
    grad_gate = jnp.dot(inputs.T.astype(jnp.float32), grad_logits.astype(jnp.float32), preferred_element_type=jnp.float32, precision=highest_precision)
    return (rounded, grad_q, grad_k, grad_v, grad_gate)

def reference(queries, keys_in, values_in, inputs, target, gate_weight, beta_bias):

    def single(sequence_parts):
        return one_sequence(*sequence_parts, gate_weight, beta_bias)
    rounded, grad_q, grad_k, grad_v, grad_gate = lax.map(single, (queries, keys_in, values_in, inputs, target))
    scaled = lax.optimization_barrier(jnp.sum(grad_gate, axis=0)) * (1.0 / math.sqrt(SEQS * SEQLEN))
    return (rounded, grad_q, grad_k, grad_v, scaled)
```

```python
import functools
import math

import jax
import jax.numpy as jnp
from jax import lax
from jax.experimental import pallas as pl
from jax.experimental.pallas import tpu as pltpu
from jax.sharding import PartitionSpec as P

EPSILON = 1e-06
HELD = True
VMEM_BYTES = 16 * 1024 * 1024

NN = (((1,), (0,)), ((), ()))
NT = (((1,), (1,)), ((), ()))
TN = (((0,), (0,)), ((), ()))

f32 = jnp.float32
bf16 = jnp.bfloat16


def split(x):
    if isinstance(x, tuple):
        return x
    if x.dtype == bf16:
        return (x,)
    head = x.astype(bf16)
    return (head, (x - head.astype(f32)).astype(bf16))


def mm(a, b, form):
    a, b = split(a), split(b)
    contract_a, contract_b = form[0][0][0], form[0][1][0]
    many_a, many_b = len(a), len(b)
    left = jnp.concatenate(a, axis=contract_a) if many_a > 1 else a[0]
    right = jnp.concatenate(b, axis=1 - contract_b) if many_b > 1 else b[0]
    if many_a > 1:
        right = jnp.concatenate([right] * many_a, axis=contract_b)
    out = lax.dot_general(left, right, form, preferred_element_type=f32)
    if many_b > 1:
        width = out.shape[1] // many_b
        out = out[:, :width] + out[:, width:]
    return out


def each(function, *lists):
    return [function(*items) for items in zip(*lists)]


def index_pair(rows, columns):
    return (
        lax.broadcasted_iota(jnp.int32, (rows, columns), 0),
        lax.broadcasted_iota(jnp.int32, (rows, columns), 1),
    )


def inverse_factor(x):
    x = x.astype(f32)
    return lax.rsqrt(jnp.sum(x * x, axis=1, keepdims=True) + EPSILON)


def head_slice(ref, head, width):
    return ref[:, head * width : (head + 1) * width]


def column(matrix, index):
    lane = lax.broadcasted_iota(jnp.int32, matrix.shape, 1)
    return jnp.sum(jnp.where(lane == index, matrix, 0.0), axis=1, keepdims=True)


def as_row(x, eye):
    return jnp.sum(jnp.where(eye, x, 0.0), axis=0, keepdims=True)


def unit_inverse(systems, length):
    row, col = index_pair(length, length)
    eye = row == col
    levels = int(math.log2(length))
    low = each(lambda a: a.astype(bf16), systems)
    solved = None
    for level in range(levels):
        same_outer = (row >> (level + 1)) == (col >> (level + 1))
        same_inner = (row >> level) == (col >> level)
        mask = same_outer & jnp.logical_not(same_inner)
        if level == 0:
            solved = each(lambda a: jnp.where(eye, 1.0, -jnp.where(mask, a, 0.0)), systems)
            continue
        known = each(lambda x: x.astype(bf16), solved)
        part = each(lambda a: jnp.where(mask, a, jnp.zeros_like(a)), low)
        middle = each(lambda a, x: mm(a, x, NN).astype(bf16), part, known)
        solved = each(lambda full, x, z: full - mm(x, z, NN), solved, known, middle)
    known = each(lambda x: x.astype(bf16), solved)
    rest = each(lambda a, x: jnp.where(eye, 1.0, 0.0) - x.astype(f32) - mm(a, x, NN), systems, known)
    return each(lambda x, r: x.astype(f32) + mm(x, r.astype(bf16), NN), known, rest)


def chronological(first, own, other):
    own, other = own.astype(f32), other.astype(f32)
    return jnp.where(first, own, other), jnp.where(first, other, own)


def both(first, own_ref, other_ref, group, width):
    pairs = [
        chronological(first, head_slice(own_ref, h, width), head_slice(other_ref, h, width))
        for h in range(group)
    ]
    return [block for pair in pairs for block in pair]


def both_strengths(step, place, first, own_ref, other_ref, group, heads):
    start = place[0] * heads + step * group
    pairs = [
        chronological(first, column(own_ref[...], start + h), column(other_ref[...], start + h))
        for h in range(group)
    ]
    return [block for pair in pairs for block in pair]


def hand_out(first, blocks, own_ref, other_ref, width):
    for h in range(len(blocks) // 2):
        early, late = blocks[2 * h : 2 * h + 2]
        columns = slice(h * width, (h + 1) * width)
        own_ref[:, columns] = jnp.where(first, early, late).astype(own_ref.dtype)
        other_ref[:, columns] = jnp.where(first, late, early).astype(other_ref.dtype)


def deliver(place, refs, share, head, pieces):
    copies, part_share = len(pieces), refs[0].shape[0]
    chips = len(refs) * part_share // share
    slot = head % share
    first = slot // part_share * chips
    for part, piece in enumerate(pieces):
        distance = lax.bitwise_xor(head * copies // share + part, place[1])
        for index, ref in enumerate(refs[first : first + chips]):

            @pl.when(distance == index)
            def _():
                ref[slot % part_share] = piece


def collect(place, refs, scratch):
    chips, part_share = scratch.shape[0], refs[0].shape[0]
    for index, ref in enumerate(refs):
        stage, distance = divmod(index, chips)
        scratch[lax.bitwise_xor(place[1], distance), stage * part_share : (stage + 1) * part_share] = ref[...]


def collected(scratch, head, copies):
    share = scratch.shape[1]
    owner = head * copies // share
    pieces = [scratch[owner + part, head % share] for part in range(copies)]
    return jnp.concatenate(pieces, axis=0) if copies > 1 else pieces[0]


def divide(place, ref, half):
    own = ref[:, pl.ds(pl.multiple_of(place[0] * half, half), half)]
    other = ref[:, pl.ds(pl.multiple_of((1 - place[0]) * half, half), half)]
    return own.astype(f32), other.astype(f32)


def pack_kernel(place, inputs, weight, bias, k, v, beta_out, send, k_out, v_out):
    half = k_out.shape[1]
    heads = weight.shape[0]
    logits = lax.dot_general(inputs[...], weight[...], NT, preferred_element_type=f32) + bias[...]
    beta = 0.5 / (1.0 + jnp.exp(-logits))
    beta_out[...] = beta
    k_out[...], send[:, :half] = divide(place, k, half)
    v_out[...], send[:, half : 2 * half] = divide(place, v, half)
    send[:, 2 * half :] = jnp.zeros((send.shape[0], send.shape[1] - 2 * half), f32)
    send[:, 2 * half : 2 * half + heads] = beta


def pack_rest_kernel(place, q, target, inputs, after, send, q_out, target_out, inputs_out):
    half = q_out.shape[1]
    q_out[...], send[:, :half] = divide(place, q, half)
    target_out[...], send[:, half : 2 * half] = divide(place, target, half)
    send[:, 2 * half :] = inputs[...].astype(f32)
    inputs_out[...] = inputs[...]


def join_kernel(place, *refs):
    count = len(refs) // 3
    first = place[0] == 0
    for index in range(count):
        own, other, out = refs[2 * index], refs[2 * index + 1], refs[2 * count + index]
        half = own.shape[1]
        early, late = chronological(first, own[...], other[...])
        out[:, :half] = early.astype(bf16)
        out[:, half:] = late.astype(bf16)


def exact(x):
    return x.astype(bf16)


def maps_kernel(
    heads, share, step, place, k, k2, v, v2, beta, beta2, early_out, late_out, early_offset_out, x_out, wk_out, wv_out, *joint_out
):
    first = place[0] == 0
    length = k.shape[0]
    group, width, _ = early_out.shape
    rows = joint_out[0].shape[1] - width
    row, col = index_pair(length, length)
    strict = row > col
    eye = row == col
    kh = both(first, k, k2, group, width)
    b = both_strengths(step, place, first, beta, beta2, group, heads)
    items = list(range(2 * group))
    rk = each(inverse_factor, kh)
    kb = each(exact, kh)
    gram = each(lambda x: mm(x, x, NT), kb)
    system = each(lambda g, b, r: jnp.where(strict, g * (b * r) * as_row(r, eye), 0.0), gram, b, rk)
    x = unit_inverse(system, length)
    wk = each(lambda x, b, r, y: mm(x * as_row(b * r, eye), y, NN), x, b, rk, kb)
    vb = each(exact, both(first, v, v2, group, width))
    wv = each(lambda x, b, y: mm(x * as_row(b, eye), y, NN), x, b, vb)
    for n in items:
        x_out[n // 2, n % 2] = x[n]
        wk_out[n // 2, n % 2] = wk[n]
        wv_out[n // 2, n % 2] = wv[n]
    maps = each(lambda a, r, b: jnp.where(eye, 1.0, 0.0) - mm(a, r * b, TN), kb, rk, wk)
    offsets = each(lambda a, r, y: mm(r * a, y, TN), wv, rk, kb)
    late = [split(maps[2 * h + 1]) for h in range(group)]
    joint = [mm(late[h], maps[2 * h], NN) for h in range(group)]
    offset = [mm(offsets[2 * h], late[h], NT) + offsets[2 * h + 1] for h in range(group)]
    for h in range(group):
        early_out[h] = maps[2 * h]
        late_out[h] = maps[2 * h + 1]
        early_offset_out[h] = offsets[2 * h]
        pieces = [
            jnp.concatenate([joint[h], offset[h][start : start + rows]], axis=0) for start in range(0, width, rows)
        ]
        deliver(place, joint_out, share, step * group + h, pieces)


def queries_kernel(step, place, q, q2, k, k2, wk, wv, early, early_offset, p_out, late_out, qj_out, oj_out):
    first = place[0] == 0
    length = q.shape[0]
    group, width, _ = late_out.shape
    row, col = index_pair(length, length)
    lower = row >= col
    items = list(range(2 * group))
    qh = both(first, q, q2, group, width)
    kh = both(first, k, k2, group, width)
    rq = each(inverse_factor, qh)
    rk = each(lambda x: as_row(inverse_factor(x), row == col), kh)
    qn = each(lambda x, r: x * r, qh, rq)
    p = each(lambda a, r, b, c: jnp.where(lower, r * mm(exact(a), exact(b), NT) * c, 0.0), qh, rq, kh, rk)
    ps = each(split, p)
    qt = [qn[n] - mm(ps[n], wk[n // 2, n % 2], NN) for n in items]
    o = [mm(ps[n], wv[n // 2, n % 2], NN) for n in items]
    for h in range(group):
        late = split(qt[2 * h + 1])
        late_out[h] = qt[2 * h + 1]
        qj_out[h, 0], oj_out[h, 0] = qt[2 * h], o[2 * h]
        qj_out[h, 1] = mm(late, early[h], NN)
        oj_out[h, 1] = o[2 * h + 1] + mm(late, early_offset[h], NT)
    for n in items:
        p_out[n // 2, n % 2] = p[n]


def scan_kernel(reverse, steps, count, place, *refs):
    *arrays, ordered_maps, ordered_offsets, states = refs
    maps, offsets, outs = arrays[:count], arrays[count:-steps], arrays[-steps:]
    share, rows, width = outs[0].shape
    heads = list(range(share))
    collect(place, maps, ordered_maps)
    if offsets:
        collect(place, offsets, ordered_offsets)
    state = [jnp.zeros((rows, width), f32) for _ in heads]
    for index in range(steps):
        n = steps - 1 - index if reverse else index
        for h in heads:
            states[n, h] = state[h]
        offset = [ordered_offsets[n, h] if offsets else ordered_maps[n, h, width:] for h in heads]
        if index == 0:
            state = offset
        elif index < steps - 1:
            form = NN if reverse else NT
            state = [mm(state[h], ordered_maps[n, h, :width], form) + offset[h] for h in heads]
    for distance in range(steps):
        outs[distance][...] = states[lax.bitwise_xor(place[1], distance)]


def output_kernel(heads, share, count, step, place, qj, oj, target, target2, *refs):
    received, refs = refs[:count], refs[count:]
    rounded_out, state_out, *g_out, ordered = refs
    first = place[0] == 0
    group, width, _ = state_out.shape

    collect(place, received, ordered)

    copies = max(1, ordered.shape[0] * ordered.shape[1] // heads)
    state = [collected(ordered, step * group + h, copies) for h in range(group)]
    items = list(range(2 * group))
    goal = both(first, target, target2, group, width)
    ts = each(split, state)
    qs = [split(qj[n // 2, n % 2]) for n in items]
    rounded = [(oj[n // 2, n % 2] + mm(qs[n], ts[n // 2], NT)).astype(bf16) for n in items]
    do = each(lambda a, b: a.astype(f32) - b, rounded, goal)
    dos = each(split, do)

    def stacked(parts, h):
        return tuple(jnp.concatenate(pair, axis=0) for pair in zip(parts[2 * h], parts[2 * h + 1]))

    joint = [mm(stacked(dos, h), stacked(qs, h), TN) for h in range(group)]
    rows = width // copies
    for h in range(group):
        pieces = [joint[h][part * rows : (part + 1) * rows] for part in range(copies)]
        deliver(place, g_out, share, step * group + h, pieces)
        state_out[h] = state[h]
    for n in items:
        rounded_out[n // 2, n % 2] = rounded[n]


def normal_pull(factor, unit, grad):
    return factor * (grad - unit * jnp.sum(unit * grad, axis=1, keepdims=True))


def fresh_kernel(
    step, place, state, early, early_offset, late, wk, wv, p, rounded, target, target2, qt_late, x, k, k2,
    mid_out, f_out, g_late_out, yp_out, xk_out, do_out, out_own, out_other,
):
    first = place[0] == 0
    group, width, _ = state.shape
    items = list(range(2 * group))
    kh = both(first, k, k2, group, width)
    rk = each(inverse_factor, kh)
    kb = each(exact, kh)
    ts = [split(state[h]) for h in range(group)]
    outs = [rounded[n // 2, n % 2].astype(f32) for n in items]
    do = each(lambda a, b: a - b, outs, both(first, target, target2, group, width))
    for n in items:
        do_out[n // 2, n % 2] = do[n]
    do = each(split, do)
    hand_out(first, outs, out_own, out_other, width)
    mid = [mm(ts[h], early[h], NT) + early_offset[h] for h in range(group)]
    g_late = [mm(do[2 * h + 1], qt_late[h], TN) for h in range(group)]
    dfp = [mm(p[n // 2, n % 2], do[n], TN) for n in items]
    ms = each(split, mid)
    f = [wv[n // 2, n % 2] - mm(wk[n // 2, n % 2], ms[n // 2] if n % 2 else ts[n // 2], NT) for n in items]
    for h in range(group):
        mid_out[h] = mid[h]
        g_late_out[h] = g_late[h]
    for n in items:
        f_out[n // 2, n % 2] = f[n]
    kj = [kb[n] if n % 2 else rk[n] * mm(kb[n], late[n // 2], NT) for n in items]
    dfp = [dfp[n] if n % 2 else dfp[n] + rk[n] * mm(kb[n], g_late[n // 2], NT) for n in items]
    xs = [x[n // 2, n % 2] for n in items]
    xk = [mm(rk[n] * xs[n] if n % 2 else xs[n], kj[n], TN) for n in items]
    yp = [mm(xs[n], dfp[n], TN) for n in items]
    for n in items:
        yp_out[n // 2, n % 2] = yp[n]
        xk_out[n // 2, n % 2] = xk[n]


def query_kernel(step, place, state, mid, f, do_all, q, q2, k, k2, gq_own, gq_other, dkp_out):
    first = place[0] == 0
    group, width, _ = state.shape
    length = q.shape[0]
    row, col = index_pair(length, length)
    lower = row >= col
    items = list(range(2 * group))
    qh = both(first, q, q2, group, width)
    rq = each(inverse_factor, qh)
    qn = each(lambda x, r: x * r, qh, rq)
    kh = both(first, k, k2, group, width)
    rk = each(lambda x: as_row(inverse_factor(x), row == col), kh)
    do = [split(do_all[n // 2, n % 2]) for n in items]
    ts = [(mid if n % 2 else state)[n // 2] for n in items]
    dp = [jnp.where(lower, mm(do[n], f[n // 2, n % 2], NT), 0.0) for n in items]
    dq = [mm(do[n], ts[n], NN) + mm(dp[n] * rk[n], exact(kh[n]), NN) for n in items]
    hand_out(first, each(normal_pull, rq, qn, dq), gq_own, gq_other, width)
    for n in items:
        dkp_out[n // 2, n % 2] = mm(rq[n] * dp[n], exact(qh[n]), TN)


def value_kernel(heads, count, step, place, yp, xk, f, beta, beta2, inputs, inputs2, *refs):
    received, refs = refs[:count], refs[count:]
    leaving_out, gw_out, dlogit, ordered = refs
    copies = max(1, ordered.shape[0] * ordered.shape[1] // heads)
    first = place[0] == 0
    group, width, _ = leaving_out.shape

    collect(place, received, ordered)

    leaving = [collected(ordered, step * group + h, copies) for h in range(group)]
    items = list(range(2 * group))
    b = both_strengths(step, place, first, beta, beta2, group, heads)
    hs = each(split, leaving)
    y = [yp[n // 2, n % 2] + mm(xk[n // 2, n % 2], hs[n // 2], NT) for n in items]

    dlogit[...] = jnp.zeros_like(dlogit)

    lane = lax.broadcasted_iota(jnp.int32, dlogit.shape[1:], 1)
    for block in range(2):
        gathered = dlogit[block]
        for h in range(group):
            n = 2 * h + block
            mine = (1.0 - 2.0 * b[n]) * jnp.sum(y[n] * f[h, block], axis=1, keepdims=True)
            gathered = gathered + jnp.where(lane == step * group + h, mine, 0.0)
        dlogit[block] = gathered
    for h in range(group):
        leaving_out[h] = leaving[h]

    own, other = chronological(first, dlogit[0], dlogit[1])
    gw_out[...] = mm(own, inputs[...], TN) + mm(other, inputs2[...].astype(bf16), TN)


def spread_kernel(scale, place, *refs):
    *parts, out = refs
    count, rows = len(parts) // 2, parts[0].shape[0]
    for side, at in ((parts[:count], place[0]), (parts[count:], 1 - place[0])):
        total = add_in_pairs([part[...] for part in side])
        out[pl.ds(pl.multiple_of(at * rows, rows), rows)] = scale * total


def add_in_pairs(parts):
    while len(parts) > 1:
        parts = [a + b for a, b in zip(parts[::2], parts[1::2])]
    return parts[0]


def key_kernel(
    heads, step, place, leaving, late, g_late, state, mid, yp, xk, f, dkp, beta, beta2, k, k2,
    gv_own, gv_other, gk_own, gk_other,
):
    first = place[0] == 0
    group, width, _ = leaving.shape
    length = k.shape[0]
    row, col = index_pair(length, length)
    strict = row > col
    items = list(range(2 * group))
    kh = both(first, k, k2, group, width)
    rk = each(inverse_factor, kh)
    kn = each(lambda x, r: x * r, kh, rk)
    fs = [split(f[n // 2, n % 2]) for n in items]
    b = both_strengths(step, place, first, beta, beta2, group, heads)
    ends = each(split, [leaving[h] for h in range(group)])
    y = [b[n] * (yp[n // 2, n % 2] + mm(xk[n // 2, n % 2], ends[n // 2], NT)) for n in items]
    hand_out(first, y, gv_own, gv_other, width)
    ys = each(split, y)
    e = [jnp.where(strict, mm(ys[n], fs[n], NT), 0.0) for n in items]
    hs = []
    for h in range(group):
        hs += [mm(ends[h], late[h], NN) + g_late[h], ends[h]]
    ts = [(mid if n % 2 else state)[n // 2] for n in items]
    dk = [dkp[n // 2, n % 2] + mm(fs[n], hs[n], NN) - mm(ys[n], ts[n], NN) for n in items]
    rows = [as_row(rk[n], row == col) for n in items]
    dk = [dk[n] - mm((e[n] + e[n].T) * rows[n], exact(kh[n]), NN) for n in items]
    hand_out(first, each(normal_pull, rk, kn, dk), gk_own, gk_other, width)


def params(products):
    return dict(
        compiler_params=pltpu.CompilerParams(vmem_limit_bytes=VMEM_BYTES),
        cost_estimate=pl.CostEstimate(flops=products * 400000000, bytes_accessed=1 << 20, transcendentals=0),
    )


def call_once(body, place, outs, operands, products):
    def whole(array):
        return pl.BlockSpec(array.shape, lambda i, c: (0,) * array.ndim)

    def shaped(shape, dtype, *held):
        return pltpu.HBM(shape, dtype) if held else jax.ShapeDtypeStruct(shape, dtype)

    arrays = [pltpu.with_memory_space_constraint(x, pltpu.HBM) if held else x for x, *held in operands]
    shapes = [shaped(*out) for out in outs]
    return pl.pallas_call(
        body,
        grid_spec=pltpu.PrefetchScalarGridSpec(
            num_scalar_prefetch=1,
            grid=(1,),
            in_specs=[whole(array) for array in arrays],
            out_specs=[whole(jax.ShapeDtypeStruct(shape, dtype)) for shape, dtype, *_ in outs],
        ),
        out_shape=shapes,
        **params(products),
    )(place, *arrays)


def call(body, place, heads, outs, operands, scratch=(), products=1):
    group, steps = heads, 1
    kinds = [kind for kind, _ in operands] + [kind for kind, _, _ in outs] + ["w"] * len(scratch)

    def view(kind, ref, step):
        if kind == "w":
            return ref
        if kind == "h":
            return ref.at[pl.ds(step * group, group)]
        columns = ref.shape[1]
        if kind == "b":
            return ref.at[:, columns - 128 :]
        if isinstance(kind, int):
            wide = 128 * group
            return ref.at[:, pl.ds(pl.multiple_of((kind * steps + step) * wide, wide), wide)]
        return ref.at[:, kind[0] : kind[1]]

    def kernel(place, *refs):
        body(0, place, *[view(kind, ref, 0) for kind, ref in zip(kinds, refs)])

    spec = pl.BlockSpec(memory_space=pltpu.VMEM)
    return pl.pallas_call(
        kernel,
        in_specs=[pl.BlockSpec(memory_space=pltpu.SMEM)] + [spec] * len(operands),
        out_specs=[spec] * len(outs),
        out_shape=[jax.ShapeDtypeStruct(shape, dtype) for _, shape, dtype in outs],
        scratch_shapes=list(scratch),
        **params(products),
    )(place, *[array for _, array in operands])


def run_scan(reverse, place, maps, offsets, shape):
    steps = lax.axis_size("chip")
    share, rows, width = shape
    spec = pl.BlockSpec(memory_space=pltpu.VMEM)
    return pl.pallas_call(
        functools.partial(scan_kernel, reverse, steps, len(maps)),
        in_specs=[pl.BlockSpec(memory_space=pltpu.SMEM)] + [spec] * (len(maps) + len(offsets)),
        out_specs=[spec] * steps,
        out_shape=[jax.ShapeDtypeStruct(shape, f32)] * steps,
        scratch_shapes=[
            pltpu.VMEM((steps, share, width + rows, width), f32),
            pltpu.VMEM((steps,) + shape, f32),
            pltpu.VMEM((steps,) + shape, f32),
        ],
        **params(1),
    )(place, *maps, *offsets)


def swapped(x, axes, distance):
    return lax.ppermute(x, axes, [(i, i ^ distance) for i in range(lax.axis_size(axes))])


def along_chips(pieces):
    came = {0: pieces[0]}
    for d in sorted(range(1, len(pieces)), key=lambda d: -d.bit_count()):
        came[d] = swapped(pieces[d], "chip", d)
    return [came[d] for d in range(len(pieces))]


def to_other_core(x):
    return lax.ppermute(x, "core", [(0, 1), (1, 0)])


def sum_with(x, fillers, place, scale):
    done = []

    def beside(came):
        if len(done) < len(fillers):
            came, outs = lax.optimization_barrier((came, fillers[len(done)](*done)))
            done.append(outs)
        return came

    chips, sequences = lax.axis_size("chip"), lax.axis_size("dp")
    base = 1
    while base < chips:
        x = add_in_pairs([x] + beside([swapped(x, "chip", d) for d in range(base, min(4 * base, chips), base)]))
        base *= 4
    distance = 1
    while distance < sequences:
        x = add_in_pairs([x] + beside([swapped(x, "dp", distance)]))
        distance *= 2
    came = [to_other_core(x)]
    for filler in fillers[len(done) :]:
        done.append(filler(*done))
    spec = pl.BlockSpec(memory_space=pltpu.VMEM)
    out = pl.pallas_call(
        functools.partial(spread_kernel, scale),
        in_specs=[pl.BlockSpec(memory_space=pltpu.SMEM)] + [spec] * (len(came) + 1),
        out_specs=spec,
        out_shape=jax.ShapeDtypeStruct((2 * x.shape[0], x.shape[1]), f32),
        **params(1),
    )(place, x, *came)
    return out.T, done


def shards(queries, keys_in, values_in, inputs, target, gate_weight, beta_bias):
    q, k, v, u, goal = queries[0], keys_in[0], values_in[0], inputs[0], target[0]
    length, model = q.shape
    all_heads = gate_weight.shape[1]
    width = model // all_heads
    heads = all_heads // 2
    half = heads * width
    places = lax.axis_size("chip")
    share = max(1, heads // places)
    copies = max(1, places // heads)
    rows = width // copies
    core = lax.axis_index("core")
    place = jnp.stack([core, lax.axis_index("chip")]).astype(jnp.int32)
    state_shape = (heads, width, width)
    square = (heads, 2, length, width)
    token_half = (length, half)
    stages = 2 if share % 2 == 0 else 1
    whole_shape = (share, rows, width)
    piece_shape = (share // stages, rows, width)
    ordered = pltpu.VMEM((places, share, rows, width), f32)
    squares = ("h", square, f32)
    states = ("h", state_shape, f32)
    halves = (0, token_half, f32)

    def by_stage(pieces):
        return [pieces[stage * places : (stage + 1) * places] for stage in range(stages)]

    with jax.named_scope("to_other_core"):
        beta, send, k_own, v_own = call_once(
            pack_kernel, place,
            [((length, all_heads), f32), ((length, 2 * half + 128), f32), (token_half, f32), (token_half, f32)],
            [(u, HELD), (gate_weight.T, HELD), (beta_bias[None], HELD), (k, HELD), (v, HELD)],
            1,
        )
        early = to_other_core(send)
    with jax.named_scope("rest_to_other_core"):
        send, q_own, goal_own, u_own = call_once(
            pack_rest_kernel, place,
            [((length, 2 * half + model), f32), (token_half, f32), (token_half, f32), (u.shape, bf16)],
            [(q, HELD), (goal, HELD), (u, HELD), (beta,)],
            6,
        )
        send, early = lax.optimization_barrier((send, early))
        rest = to_other_core(send)
    keys = [(0, k_own), (0, early)]
    strengths = [("w", beta), ("b", early)]
    with jax.named_scope("chip_maps"):
        early_map, late_map, early_offset, x, wk, wv, *joint = call(
            functools.partial(maps_kernel, heads, share), place, heads,
            [states] * 3 + [squares] * 3 + [("w", (share // stages, width + rows, width), f32)] * (places * stages),
            keys + [(0, v_own), (1, early)] + strengths,
            products=16,
        )
    with jax.named_scope("maps_to_owners"):
        joint, rest = lax.optimization_barrier((joint, rest))
        maps = [along_chips(part) for part in by_stage(joint)]
    with jax.named_scope("query_terms"):
        p, qt_late, qj, oj = call(
            queries_kernel, place, heads,
            [squares, states] + [squares] * 2,
            [(0, q_own), (0, rest)] + keys + [("h", wk), ("h", wv), ("h", early_map), ("h", early_offset)],
            products=4,
        )
    with jax.named_scope("forward_recurrence"):
        received, states_of = [], None
        for part in maps:
            if states_of is not None:
                part = lax.optimization_barrier((part, states_of))[0]
            states_of = run_scan(False, place, part, [], piece_shape)
            received += along_chips(states_of)
    with jax.named_scope("outputs"):
        rounded, state, *g = call(
            functools.partial(output_kernel, heads, share, places * stages), place, heads,
            [("h", square, bf16), states] + [("w", whole_shape, f32)] * places,
            [("h", qj), ("h", oj), (0, goal_own), (1, rest)] + [("w", piece) for piece in received],
            [ordered],
            products=3,
        )
    with jax.named_scope("cotangents_to_owners"):
        g = along_chips(g)
    with jax.named_scope("fresh_terms"):
        mid, f, g_late, yp, xk, do, out_own, out_other = call(
            fresh_kernel, place, heads,
            [states, squares, states] + [squares] * 3 + [halves] * 2,
            [("h", state), ("h", early_map), ("h", early_offset), ("h", late_map), ("h", wk), ("h", wv)]
            + [("h", p), ("h", rounded), (0, goal_own), (1, rest), ("h", qt_late), ("h", x)] + keys,
            products=8,
        )
        g, f = lax.optimization_barrier((g, f))
    with jax.named_scope("query_gradients"):
        gq_own, gq_other, dkp = call(
            query_kernel, place, heads,
            [halves] * 2 + [squares],
            [("h", state), ("h", mid), ("h", f), ("h", do), (0, q_own), (0, rest)] + keys,
            products=6,
        )
        out_other, gq_other = lax.optimization_barrier((out_other, gq_other))
        out_other, gq_other = to_other_core(out_other), to_other_core(gq_other)
    with jax.named_scope("backward_recurrence"):
        received = along_chips(run_scan(True, place, [piece for part in maps for piece in part], g, whole_shape))
    with jax.named_scope("value_gradients"):
        leaving, gw = call(
            functools.partial(value_kernel, heads, places), place, heads,
            [states, ("w", (heads, model), f32)],
            [("h", yp), ("h", xk), ("h", f)] + strengths
            + [("w", u_own), ((model, 2 * model), rest)]
            + [("w", piece) for piece in received],
            [pltpu.VMEM((2, length, heads), f32), ordered],
            products=3,
        )

    def key_gradients():
        return call(
            functools.partial(key_kernel, heads), place, heads,
            [halves] * 4,
            [("h", leaving), ("h", late_map), ("h", g_late), ("h", state), ("h", mid)]
            + [("h", yp), ("h", xk), ("h", f), ("h", dkp)] + strengths + keys,
            products=6,
        )

    def joined(*halves):
        return call_once(
            join_kernel, place, [((length, model), bf16, HELD)] * (len(halves) // 2), [(x,) for x in halves], 20
        )

    with jax.named_scope("weight_and_key_gradients"):
        gw, (_, (out, gq), (gv, gk)) = sum_with(
            gw,
            [
                key_gradients,
                lambda _: joined(out_own, out_other, gq_own, gq_other),
                lambda grads, _: joined(grads[0], to_other_core(grads[1]), grads[2], to_other_core(grads[3])),
            ],
            place,
            1.0 / math.sqrt(length * 2 * places * lax.axis_size("dp")),
        )
    return (out[None], gq[None], gk[None], gv[None], gw)


def solution(mesh):
    seq, dp = mesh.shape["seq"], mesh.shape["dp"]
    cut = jax.sharding.Mesh(mesh.devices.reshape(seq // 2, 2, dp), ("chip", "core", "dp"))
    split_tokens = P("dp", ("chip", "core"), None)
    return jax.shard_map(
        shards,
        mesh=cut,
        in_specs=(split_tokens,) * 5 + (P(), P()),
        out_specs=(split_tokens,) * 4 + (P(),),
        check_vma=False,
    )
```
